32 devices in a mesh: groups: 2 (over y), seq: 4 (over z), heads: 4 (over x, core).
Axes of the slice: x: 2, y: 2, z: 4, core: 2. Of those that a mesh axis runs over, the one named last changes fastest.
Arguments:
- prompt_token_input: bfloat16 [8, 256, 4096], P('groups', 'heads', 'seq'), parts along dimension 0, may hold values from -6 to 6
- lengths: int32 [8], P('groups'), parts along dimension 0, may hold values from 1 to 256, 512 in all
- request_adapter_index: int32 [8], P('groups'), parts along dimension 0, may hold values from 0 to 7
- assignment: int32 [8], P('groups'), parts along dimension 0, may hold values from 0 to 3, each once
- encoder_gate_weight: bfloat16 [4096, 5120], P(None, 'seq'), may hold values from -0.09375 to 0.09375
- encoder_up_weight: bfloat16 [4096, 5120], P(None, 'seq'), may hold values from -0.09375 to 0.09375
- encoder_down_weight: bfloat16 [5120, 4096], P('seq'), may hold values from -0.125 to 0.125
- adapter_down_maps: bfloat16 [8, 4096, 16], replicated, may hold values from -0.09375 to 0.09375
- adapter_up_maps: bfloat16 [8, 16, 5120], P(None, None, 'seq'), may hold values from -1.5 to 1.5
- text_key_value_weight: bfloat16 [4096, 2, 3072], P('seq', None, 'heads'), may hold values from -0.09375 to 0.09375
- image_token_activations: bfloat16 [8, 1024, 3072], P(('groups', 'seq'), 'heads'), parts along dimension 0, may hold values from -6 to 6
- modulation: bfloat16 [8, 2, 3072], P(('groups', 'seq')), parts along dimension 0, may hold values from -2.5 to 2.5
- image_query_key_value_weight: bfloat16 [3072, 3, 3072], P('seq', None, 'heads'), may hold values from -0.109375 to 0.109375
- query_key_norm_gain: float32 [3, 24, 128], P(None, 'heads'), may hold values from 0.5 to 2.5
Outputs:
- attended: bfloat16 [8, 1024, 3072], P(('groups', 'seq'), None, 'heads'), parts along dimension 0
The draws below stay inside these ranges and needn't reach their ends.
There are 2 independent parts, one for each index of `groups`. The reference program is written for one: setup_inputs(seed, part) draws one part's arguments, and reference() takes and returns one part's arrays. A program takes and returns all parts, laid end to end along the dimension named above; an argument that names none is the same for every part. Nothing has to cross between parts.
Inputs may be any that keep to these rules, and one draw needn't show every extreme that they name: `lengths`: the longest prompt has exactly 256 tokens. `assignment`: every image index is assigned exactly one request.
All inputs are finite; a program needn't handle non-finite values.
Results may differ from the reference program's by a relative error of at most 0.014.
Values may be sent and summed in bfloat16 or wider, within the bound.
A program may use at most 192 MiB of HBM per device.

```python
import math
import jax
import jax.numpy as jnp
import numpy as np
from jax import lax

ENCODER_WIDTH = 4096
FEEDFWD_UNITS = 5120
ADAPTER_RANK = 16
ADAPTER_COUNT = 8
LTXT = 256
W = 3072
HEADS = 24
HD = 128
IMG = 1024
REQ = 4
N_SEQ = 4


def draw_query_key_norm_gain(key, part):
    key = jax.random.fold_in(key, 17)
    entry_key = jax.random.fold_in(key, 1)
    return jax.random.uniform(entry_key, (3, HEADS, HD), jnp.float32, 0.5, 1.5)


def place_ends(drawn, stream_key, low, largest):
    extent = drawn.shape
    place = [jax.random.randint(jax.random.fold_in(stream_key, axis), (), 0, extent[axis]) for axis in range(len(extent))]
    drawn = drawn.at[tuple(place)].set(low)
    longest = extent.index(max(extent))
    place[longest] = (place[longest] + 1) % extent[longest]
    return drawn.at[tuple(place)].set(largest)


def raised(values, own_key, source, target, blocks, factor):
    def block_of(position):
        return (jnp.arange(values.shape[position]) // (values.shape[position] // blocks)).reshape((-1,) + (1,) * (values.ndim - 1 - position))

    first = jax.random.permutation(own_key, blocks)[block_of(target)]
    second = (block_of(target) + blocks // 2) % blocks
    return jnp.where((block_of(source) == first) | (block_of(source) == second), factor * values, values)


def levels(stream_key, dims, cuts, smallest, top_value):
    def one(position, blocks):
        heights = jax.random.uniform(jax.random.fold_in(jax.random.fold_in(stream_key, 6), position), (blocks,), jnp.float32, smallest / len(cuts), top_value / len(cuts))
        return jnp.repeat(jnp.exp(heights), dims[position] // blocks).reshape((-1,) + (1,) * (len(dims) - position - 1))

    level = one(*cuts[0])
    for cut in cuts[1:]:
        level = level * one(*cut)
    return level


def length_profile(number_of, total, reach, skew):
    loads = [(1 << 20) // math.isqrt(rank ** skew) + 1 for rank in range(2, number_of + 1)]
    spare, holding = total - reach - (number_of - 1), [1] * (number_of - 1)
    while spare > 0:
        movable = [i for i in range(number_of - 1) if holding[i] < reach]
        whole, left = sum([loads[i] for i in movable]), spare
        for i in movable:
            addition = min(reach - holding[i], max(1, left * loads[i] // whole), spare)
            holding[i] = holding[i] + addition
            spare = spare - addition
    return np.array([reach] + holding)


def uneven(stream_key, count, total, reach, skew):
    if count == 2:
        one = jax.random.randint(stream_key, (), max(1, total - reach), min(reach, total - 1) + 1)
        return jnp.stack([one, total - one])
    sizes = jnp.asarray(length_profile(count, total, reach, skew), jnp.int32)
    pairs = (count - 1) // 2
    giver, taker = sizes[1:1 + 2 * pairs:2], sizes[2:2 + 2 * pairs:2]
    room = jnp.minimum(giver - 1, reach - taker)
    passed = jax.random.randint(jax.random.fold_in(stream_key, 1), (pairs,), 0, 1 << 20) % (room + 1)
    sizes = sizes.at[1:1 + 2 * pairs:2].set(giver - passed).at[2:2 + 2 * pairs:2].set(taker + passed)
    return sizes[jax.random.permutation(jax.random.fold_in(stream_key, 2), count)]


def scatter_about(key, dims, deviation, bound, cuts=(), kind=jnp.bfloat16):
    loudness = levels(key, dims, cuts, -0.22, 0.18) if cuts else 1.0
    result = jax.random.normal(key, dims, jnp.float32) * deviation * loudness
    return jnp.minimum(jnp.maximum(result, -bound), bound).astype(kind)


def bell_draw_with(key, dims, scale, bound, cuts, heavy, held_as=jnp.bfloat16):
    result = scale * jax.random.normal(key, dims, jnp.float32)
    if cuts:
        result = result * levels(key, dims, cuts, -0.22, 0.18)
    return jnp.clip(raised(result, jax.random.fold_in(key, 3), *heavy), -bound, bound).astype(held_as)


def setup_inputs(seed: int = 0, part: int = 0) -> dict:
    seeds = jax.random.split(jax.random.key(seed), 15)
    own_keys = jax.random.split(jax.random.fold_in(seeds[14], part), 15)
    prompt_token_input = scatter_about(own_keys[0], (REQ, LTXT, ENCODER_WIDTH), 1.0, 6.0, ((1, 4), (2, 4)))
    lengths = uneven(own_keys[1], REQ, REQ * LTXT // 2, LTXT, 2).astype(jnp.int32)
    request_adapter_index = place_ends(jax.random.randint(own_keys[2], (REQ,), 0, ADAPTER_COUNT), jax.random.fold_in(own_keys[2], 1), 0, ADAPTER_COUNT - 1).astype(jnp.int32)
    assignment = jax.random.permutation(own_keys[3], REQ).astype(jnp.int32)
    encoder_gate_weight = scatter_about(seeds[4], (ENCODER_WIDTH, FEEDFWD_UNITS), ENCODER_WIDTH ** -0.5, 0.09375, ((1, 4),))
    encoder_up_weight = scatter_about(seeds[5], (ENCODER_WIDTH, FEEDFWD_UNITS), ENCODER_WIDTH ** -0.5, 0.09375, ((1, 4),))
    encoder_down_weight = bell_draw_with(seeds[6], (FEEDFWD_UNITS, ENCODER_WIDTH), FEEDFWD_UNITS ** -0.5, 0.125, ((0, 4),), (0, 1, 4, 2.0))
    adapter_down_maps = scatter_about(seeds[7], (ADAPTER_COUNT, ENCODER_WIDTH, ADAPTER_RANK), ENCODER_WIDTH ** -0.5, 0.09375)
    adapter_up_maps = scatter_about(seeds[8], (ADAPTER_COUNT, ADAPTER_RANK, FEEDFWD_UNITS), ADAPTER_RANK ** -0.5, 1.5, ((2, 4),))
    text_key_value_weight = scatter_about(seeds[9], (ENCODER_WIDTH, 2, W), ENCODER_WIDTH ** -0.5, 0.09375, ((0, 4), (2, 4)))
    image_token_activations = scatter_about(own_keys[10], (REQ, IMG, W), 1.0, 6.0, ((0, 4), (1, 4)))
    modulation = scatter_about(own_keys[11], (REQ, 2, W), 0.4, 2.5, ((0, 4),))
    image_query_key_value_weight = scatter_about(seeds[12], (W, 3, W), W ** -0.5, 0.109375, ((0, 4), (2, 4)))
    query_key_norm_gain = draw_query_key_norm_gain(jax.random.fold_in(seeds[14], 71), part)
    return {"prompt_token_input": prompt_token_input, "lengths": lengths, "request_adapter_index": request_adapter_index, "assignment": assignment, "encoder_gate_weight": encoder_gate_weight, "encoder_up_weight": encoder_up_weight, "encoder_down_weight": encoder_down_weight, "adapter_down_maps": adapter_down_maps, "adapter_up_maps": adapter_up_maps, "text_key_value_weight": text_key_value_weight, "image_token_activations": image_token_activations, "modulation": modulation, "image_query_key_value_weight": image_query_key_value_weight, "query_key_norm_gain": query_key_norm_gain}


eps_norm = 1e-06
adapter_scale = 0.5
neg_fill = -1e+30

def rms_rows(values):
    return values * lax.rsqrt(lax.optimization_barrier(jnp.mean(values * values, axis=-1, keepdims=True)) + eps_norm)

def attend(queries, image_keys, image_values, text_keys, text_values, live_mask):
    factor = 1.0 / math.sqrt(queries.shape[-1])
    query_wide = queries.astype(jnp.float32)
    image_scores = jnp.einsum('qhd,khd->hqk', query_wide, image_keys.astype(jnp.float32)) * factor
    text_scores = jnp.einsum('qhd,khd->hqk', query_wide, text_keys.astype(jnp.float32)) * factor
    text_scores = jnp.where(live_mask[None, None, :], text_scores, neg_fill)
    scores = jnp.concatenate([image_scores, text_scores], axis=2)
    row_max = lax.optimization_barrier(jnp.max(scores, axis=2, keepdims=True))
    weights = jnp.exp(scores - row_max)
    shares = (weights / lax.optimization_barrier(jnp.sum(weights, axis=2, keepdims=True))).astype(jnp.bfloat16)
    values = jnp.concatenate([image_values, text_values], axis=0)
    return jnp.einsum('hqk,khd->qhd', shares.astype(jnp.float32), values.astype(jnp.float32)).astype(jnp.bfloat16)

def reference(prompt_token_input, lengths, request_adapter_index, assignment, encoder_gate_weight, encoder_up_weight, encoder_down_weight, adapter_down_maps, adapter_up_maps, text_key_value_weight, image_token_activations, modulation, image_query_key_value_weight, query_key_norm_gain):
    requests, positions, width = prompt_token_input.shape
    floated = prompt_token_input.astype(jnp.float32)
    normed = rms_rows(floated).astype(jnp.bfloat16)
    selected_down_maps = adapter_down_maps[request_adapter_index]
    selected_up_maps = adapter_up_maps[request_adapter_index]
    adapter_projected = jnp.einsum('rpd,rdk->rpk', normed.astype(jnp.float32), selected_down_maps.astype(jnp.float32)).astype(jnp.bfloat16)
    flattened = normed.reshape(requests * positions, width)
    gated_hidden = jnp.dot(flattened, encoder_gate_weight, preferred_element_type=jnp.float32).reshape(requests, positions, FEEDFWD_UNITS)
    gated_hidden = gated_hidden + adapter_scale * jnp.einsum('sqt,sti->sqi', adapter_projected.astype(jnp.float32), selected_up_maps.astype(jnp.float32))
    up_proj = jnp.dot(flattened, encoder_up_weight, preferred_element_type=jnp.float32).reshape(requests, positions, FEEDFWD_UNITS)
    hidden = (jax.nn.gelu(gated_hidden, approximate=True) * up_proj).astype(jnp.bfloat16).reshape(requests * positions, FEEDFWD_UNITS)
    block_width = FEEDFWD_UNITS // N_SEQ
    running = jnp.zeros((requests * positions, width), jnp.float32)
    for block_index in range(N_SEQ):
        lower = block_index * block_width
        part_sum = jnp.dot(hidden[:, lower:lower + block_width], encoder_down_weight[lower:lower + block_width], preferred_element_type=jnp.float32)
        running = running + lax.optimization_barrier(part_sum.astype(jnp.bfloat16)).astype(jnp.float32)
    encoded = (floated.reshape(requests * positions, width) + running).astype(jnp.bfloat16).reshape(requests, positions, width)
    slots = jnp.arange(requests, dtype=jnp.int32)
    prompt_order = lax.optimization_barrier(jnp.sum(slots[None, :] * (assignment[None, :] == slots[:, None]).astype(jnp.int32), axis=1)).astype(jnp.int32)
    heads_total = query_key_norm_gain.shape[1]
    head_dim = query_key_norm_gain.shape[2]
    kv_flat = text_key_value_weight.reshape(width, -1)
    qkv_flat = image_query_key_value_weight.reshape(image_query_key_value_weight.shape[0], -1)
    image_count = image_token_activations.shape[1]

    def one_image(image_slot):
        source_row = prompt_order[image_slot]
        prompt = encoded[source_row]
        live_length = lengths[source_row]
        text_proj = jnp.dot(prompt, kv_flat, preferred_element_type=jnp.float32).reshape(positions, 2, heads_total, head_dim)
        text_keys = (rms_rows(text_proj[:, 0]) * query_key_norm_gain[2]).astype(jnp.bfloat16)
        text_values = text_proj[:, 1].astype(jnp.bfloat16)
        pixels = image_token_activations[image_slot].astype(jnp.float32)
        row_mean = lax.optimization_barrier(jnp.mean(pixels, axis=-1, keepdims=True))
        centered = pixels - row_mean
        normal_rows = centered * lax.rsqrt(lax.optimization_barrier(jnp.mean(centered * centered, axis=-1, keepdims=True)) + eps_norm)
        shift_row = modulation[image_slot, 0].astype(jnp.float32)
        scale_row = modulation[image_slot, 1].astype(jnp.float32)
        modulated = (normal_rows * (1.0 + scale_row) + shift_row).astype(jnp.bfloat16)
        image_proj = jnp.dot(modulated, qkv_flat, preferred_element_type=jnp.float32).reshape(image_count, 3, heads_total, head_dim)
        image_queries = (rms_rows(image_proj[:, 0]) * query_key_norm_gain[0]).astype(jnp.bfloat16)
        image_keys = (rms_rows(image_proj[:, 1]) * query_key_norm_gain[1]).astype(jnp.bfloat16)
        image_values = image_proj[:, 2].astype(jnp.bfloat16)
        live_mask = jnp.arange(positions, dtype=jnp.int32) < live_length
        output = attend(image_queries, image_keys, image_values, text_keys, text_values, live_mask)
        return output.reshape(image_count, heads_total * head_dim)
    return lax.map(one_image, slots)
```

```python
import functools
import math

import jax
import jax.numpy as jnp
from jax import lax
from jax.experimental import pallas as pl
from jax.experimental.pallas import tpu as pltpu
from jax.sharding import PartitionSpec as P

eps_norm = 1e-06
adapter_scale = 0.5
neg_fill = -1e30


def rms_rows(values):
    return values * lax.rsqrt(jnp.mean(values * values, axis=-1, keepdims=True) + eps_norm)


def line_plan(count):
    plan = []
    for place in range(count):
        found = []
        for steps in range(1, count):
            pair = [(place + steps, "down"), (place - steps, "up")]
            if place >= count // 2:
                pair.reverse()
            found += [(source, way, steps) for source, way in pair if 0 <= source < count]
        plan.append(found)
    return plan


def chunk_product(tokens, weight):
    return [
        jnp.dot(tokens, weight[j], preferred_element_type=jnp.float32)
        for j in range(weight.shape[0])
    ]


def added(left, right):
    return [a + b for a, b in zip(left, right)]


def attention_kernel(
    live_ref, gain_ref, query_ref, key_ref, value_ref, text_key_ref, text_value_ref, out_ref,
    *, rows_per_step
):
    head_dim = query_ref.shape[1]
    factor = 1.0 / math.sqrt(head_dim)
    live = live_ref[0]
    image_keys = (rms_rows(key_ref[...]) * gain_ref[0, 1][None, :]).astype(jnp.bfloat16)
    text_keys = (
        rms_rows(text_key_ref[...].astype(jnp.float32)) * gain_ref[0, 2][None, :]
    ).astype(jnp.bfloat16)
    image_values = value_ref[...].astype(jnp.bfloat16)
    text_values = text_value_ref[...].astype(jnp.bfloat16)
    text_count = text_keys.shape[0]
    contract = (((1,), (1,)), ((), ()))
    for start in range(0, query_ref.shape[0], rows_per_step):
        rows = pl.ds(start, rows_per_step)
        queries = (rms_rows(query_ref[rows, :]) * gain_ref[0, 0][None, :]).astype(jnp.bfloat16)
        image_scores = lax.dot_general(
            queries, image_keys, contract, preferred_element_type=jnp.float32
        )
        text_scores = lax.dot_general(
            queries, text_keys, contract, preferred_element_type=jnp.float32
        )
        image_weights = jnp.exp(image_scores * factor)
        position = lax.broadcasted_iota(jnp.int32, (rows_per_step, text_count), 1)
        text_weights = jnp.where(position < live, jnp.exp(text_scores * factor), 0.0)
        total = jnp.sum(image_weights, axis=1, keepdims=True) + jnp.sum(
            text_weights, axis=1, keepdims=True
        )
        inverse = 1.0 / total
        attended = jnp.dot(
            (image_weights * inverse).astype(jnp.bfloat16),
            image_values,
            preferred_element_type=jnp.float32,
        ) + jnp.dot(
            (text_weights * inverse).astype(jnp.bfloat16),
            text_values,
            preferred_element_type=jnp.float32,
        )
        out_ref[rows, :] = attended.astype(out_ref.dtype)


def attention(live_length, gain, queries, keys, values, text):
    image_count, columns = queries.shape
    head_dim = gain.shape[2]
    heads_here = columns // head_dim
    text_count = text.shape[0]

    def image_block():
        return pl.BlockSpec((image_count, head_dim), lambda h: (0, h))

    rows_per_step = math.gcd(image_count, 256)
    pairs = image_count * (image_count + text_count) * heads_here
    return pl.pallas_call(
        functools.partial(attention_kernel, rows_per_step=rows_per_step),
        grid=(heads_here,),
        in_specs=[
            pl.BlockSpec(memory_space=pltpu.SMEM),
            pl.BlockSpec((1, 3, head_dim), lambda h: (h, 0, 0)),
            image_block(),
            image_block(),
            image_block(),
            pl.BlockSpec((text_count, head_dim), lambda h: (0, h)),
            pl.BlockSpec((text_count, head_dim), lambda h: (0, heads_here + h)),
        ],
        out_specs=image_block(),
        out_shape=jax.ShapeDtypeStruct((image_count, columns), jnp.bfloat16),
        compiler_params=pltpu.CompilerParams(vmem_limit_bytes=40 * 1024 * 1024),
        cost_estimate=pl.CostEstimate(
            flops=4 * pairs * head_dim,
            bytes_accessed=14 * image_count * columns + 4 * text_count * columns,
            transcendentals=pairs,
        ),
    )(live_length.reshape(1), gain.transpose(1, 0, 2), queries, keys, values, text, text)


def modulated_rows(image_token_activations, modulation):
    pixels = image_token_activations[0].astype(jnp.float32)
    row_mean = jnp.mean(pixels, axis=-1, keepdims=True)
    centered = pixels - row_mean
    normal_rows = centered * lax.rsqrt(
        jnp.mean(centered * centered, axis=-1, keepdims=True) + eps_norm
    )
    shift_row = modulation[0, 0].astype(jnp.float32)
    scale_row = modulation[0, 1].astype(jnp.float32)
    return (normal_rows * (1.0 + scale_row) + shift_row).astype(jnp.bfloat16)


def image_part(image_token_activations, modulation, image_weight):
    replicas = lax.axis_size("groups")
    count = lax.axis_size("seq")
    my_replica = lax.axis_index("groups")
    place = lax.axis_index("seq")
    modulated = modulated_rows(image_token_activations, modulation)
    full_image = lax.all_gather(modulated, "heads", axis=0, tiled=True)
    depth = image_weight.shape[0]
    share = depth // replicas
    own = image_weight.transpose(1, 0, 2)
    piece = lax.dynamic_slice_in_dim(own, my_replica * share, share, 1)

    def tokens_of(first, length):
        return lax.dynamic_slice_in_dim(full_image, first, length, 1)

    plan = line_plan(count)
    going_up = [(i, i + 1) for i in range(count - 1)]
    going_down = [(i + 1, i) for i in range(count - 1)]
    up, down = [piece], [piece]
    total = chunk_product(tokens_of(place * depth, depth), own)
    for step in range(1, count):
        up.append(lax.ppermute(up[-1], "seq", going_up))
        down.append(lax.ppermute(down[-1], "seq", going_down))
        choices = {}
        for here in range(count):
            source, way, steps = plan[here][step - 1]
            choices.setdefault((way, steps), []).append(here)
        chosen = None
        for (way, steps), places in choices.items():
            array = (up if way == "up" else down)[steps]
            if chosen is None:
                chosen = array
            else:
                here = functools.reduce(jnp.logical_or, [place == i for i in places])
                chosen = jnp.where(here, array, chosen)
        source = jnp.array([plan[here][step - 1][0] for here in range(count)], jnp.int32)[place]
        chosen = lax.optimization_barrier(chosen)
        total = added(
            total, chunk_product(tokens_of(source * depth + my_replica * share, share), chosen)
        )
        for turn in range(1, replicas):
            theirs = lax.ppermute(
                chosen, "groups", [((i + turn) % replicas, i) for i in range(replicas)]
            )
            replica = lax.rem(my_replica + turn, replicas)
            total = added(
                total, chunk_product(tokens_of(source * depth + replica * share, share), theirs)
            )
    return total


def local(
    prompt_token_input,
    lengths,
    request_adapter_index,
    assignment,
    encoder_gate_weight,
    encoder_up_weight,
    encoder_down_weight,
    adapter_down_maps,
    adapter_up_maps,
    text_key_value_weight,
    image_token_activations,
    modulation,
    image_query_key_value_weight,
    query_key_norm_gain,
):
    requests = prompt_token_input.shape[0]
    positions = prompt_token_input.shape[1]
    my_slot = lax.axis_index("seq")
    whole = lax.all_gather(prompt_token_input, "seq", axis=2, tiled=True)
    image_proj = image_part(image_token_activations, modulation, image_query_key_value_weight)
    width = whole.shape[2]
    normed = rms_rows(whole.astype(jnp.float32)).astype(jnp.bfloat16)
    tenant_adapters = adapter_down_maps.shape[0]
    selected_adapter = (
        request_adapter_index[:, None] == jnp.arange(tenant_adapters, dtype=jnp.int32)[None, :]
    ).astype(jnp.bfloat16)
    selected_down_maps = jnp.einsum(
        "mn,nhi->mhi", selected_adapter, adapter_down_maps, preferred_element_type=jnp.float32
    ).astype(jnp.bfloat16)
    selected_up_maps = jnp.einsum(
        "zl,log->zog", selected_adapter, adapter_up_maps, preferred_element_type=jnp.float32
    ).astype(jnp.bfloat16)
    adapter_projected = jnp.einsum(
        "rpd,rdk->rpk", normed, selected_down_maps, preferred_element_type=jnp.float32
    ).astype(jnp.bfloat16)
    flattened = normed.reshape(requests * positions, width)
    gated_hidden = jnp.dot(
        flattened, encoder_gate_weight, preferred_element_type=jnp.float32
    ).reshape(requests, positions, -1)
    gated_hidden = gated_hidden + adapter_scale * jnp.einsum(
        "sqt,sti->sqi", adapter_projected, selected_up_maps, preferred_element_type=jnp.float32
    )
    up_proj = jnp.dot(flattened, encoder_up_weight, preferred_element_type=jnp.float32).reshape(
        requests, positions, -1
    )
    hidden = (jax.nn.gelu(gated_hidden, approximate=True) * up_proj).astype(jnp.bfloat16)
    slots = jnp.arange(requests, dtype=jnp.int32)
    prompt_order = jnp.sum(
        slots[None, :] * (assignment[None, :] == slots[:, None]).astype(jnp.int32), axis=1
    )
    source_row = prompt_order[my_slot]
    live_length = lengths[source_row]
    partial = jnp.einsum(
        "rpf,fd->rpd", hidden, encoder_down_weight, preferred_element_type=jnp.float32
    ).astype(jnp.bfloat16)
    summed = lax.psum_scatter(partial, "seq", scatter_dimension=2, tiled=True)
    encoded = (
        summed.astype(jnp.float32) + prompt_token_input.astype(jnp.float32)
    ).astype(jnp.bfloat16)
    prompts = lax.all_gather(encoded, "heads", axis=1, tiled=True)
    text_count = prompts.shape[1]
    ordered = jnp.take(prompts, prompt_order, axis=0).reshape(requests * text_count, -1)
    text_partial = jnp.concatenate(
        [
            jnp.dot(
                ordered, text_key_value_weight[:, j], preferred_element_type=jnp.float32
            ).astype(jnp.bfloat16)
            for j in range(2)
        ],
        axis=1,
    ).reshape(requests, text_count, -1)
    text = lax.psum_scatter(text_partial, "seq", scatter_dimension=0, tiled=True)[0]
    output = attention(
        live_length, query_key_norm_gain, image_proj[0], image_proj[1], image_proj[2], text
    )
    return output[None]


def solution(mesh):
    return jax.shard_map(
        local,
        mesh=mesh,
        in_specs=(
            P("groups", "heads", "seq"),
            P("groups"),
            P("groups"),
            P("groups"),
            P(None, "seq"),
            P(None, "seq"),
            P("seq", None),
            P(),
            P(None, None, "seq"),
            P("seq", None, "heads"),
            P(("groups", "seq"), "heads", None),
            P(("groups", "seq"), None, None),
            P("seq", None, "heads"),
            P(None, "heads", None),
        ),
        out_specs=P(("groups", "seq"), None, "heads"),
        check_vma=False,
    )
```

```python
import functools
import math

import jax
import jax.numpy as jnp
from jax import lax
from jax.experimental import pallas as pl
from jax.experimental.pallas import tpu as pltpu
from jax.sharding import PartitionSpec as P

eps_norm = 1e-06
adapter_scale = 0.5
neg_fill = -1e30


def rms_rows(values):
    return values * lax.rsqrt(jnp.mean(values * values, axis=-1, keepdims=True) + eps_norm)


def line_plan(count):
    plan = []
    for place in range(count):
        found = []
        for steps in range(1, count):
            pair = [(place + steps, "down"), (place - steps, "up")]
            if place >= count // 2:
                pair.reverse()
            found += [(source, way, steps) for source, way in pair if 0 <= source < count]
        plan.append(found)
    return plan


def attention_kernel(
    live_ref, gain_ref, query_ref, key_ref, value_ref, text_key_ref, text_value_ref, out_ref,
    *, rows_per_step
):
    head_dim = query_ref.shape[1]
    factor = 1.0 / math.sqrt(head_dim)
    live = live_ref[0]
    image_keys = (rms_rows(key_ref[...]) * gain_ref[0, 1][None, :]).astype(jnp.bfloat16)
    text_keys = (
        rms_rows(text_key_ref[...].astype(jnp.float32)) * gain_ref[0, 2][None, :]
    ).astype(jnp.bfloat16)
    image_values = value_ref[...].astype(jnp.bfloat16)
    text_values = text_value_ref[...].astype(jnp.bfloat16)
    text_count = text_keys.shape[0]
    contract = (((1,), (1,)), ((), ()))
    for start in range(0, query_ref.shape[0], rows_per_step):
        rows = pl.ds(start, rows_per_step)
        queries = (rms_rows(query_ref[rows, :]) * gain_ref[0, 0][None, :]).astype(jnp.bfloat16)
        image_scores = lax.dot_general(
            queries, image_keys, contract, preferred_element_type=jnp.float32
        )
        text_scores = lax.dot_general(
            queries, text_keys, contract, preferred_element_type=jnp.float32
        )
        image_weights = jnp.exp(image_scores * factor)
        position = lax.broadcasted_iota(jnp.int32, (rows_per_step, text_count), 1)
        text_weights = jnp.where(position < live, jnp.exp(text_scores * factor), 0.0)
        total = jnp.sum(image_weights, axis=1, keepdims=True) + jnp.sum(
            text_weights, axis=1, keepdims=True
        )
        inverse = 1.0 / total
        attended = jnp.dot(
            (image_weights * inverse).astype(jnp.bfloat16),
            image_values,
            preferred_element_type=jnp.float32,
        ) + jnp.dot(
            (text_weights * inverse).astype(jnp.bfloat16),
            text_values,
            preferred_element_type=jnp.float32,
        )
        out_ref[rows, :] = attended.astype(out_ref.dtype)


def attention(live_length, gain, queries, keys, values, text):
    image_count, columns = queries.shape
    head_dim = gain.shape[2]
    heads_here = columns // head_dim
    text_count = text.shape[0]

    def image_block():
        return pl.BlockSpec((image_count, head_dim), lambda h: (0, h))

    rows_per_step = math.gcd(image_count, 256)
    pairs = image_count * (image_count + text_count) * heads_here
    return pl.pallas_call(
        functools.partial(attention_kernel, rows_per_step=rows_per_step),
        grid=(heads_here,),
        in_specs=[
            pl.BlockSpec(memory_space=pltpu.SMEM),
            pl.BlockSpec((1, 3, head_dim), lambda h: (h, 0, 0)),
            image_block(),
            image_block(),
            image_block(),
            pl.BlockSpec((text_count, head_dim), lambda h: (0, h)),
            pl.BlockSpec((text_count, head_dim), lambda h: (0, heads_here + h)),
        ],
        out_specs=image_block(),
        out_shape=jax.ShapeDtypeStruct((image_count, columns), jnp.bfloat16),
        compiler_params=pltpu.CompilerParams(vmem_limit_bytes=40 * 1024 * 1024),
        cost_estimate=pl.CostEstimate(
            flops=4 * pairs * head_dim,
            bytes_accessed=14 * image_count * columns + 4 * text_count * columns,
            transcendentals=pairs,
        ),
    )(live_length.reshape(1), gain.transpose(1, 0, 2), queries, keys, values, text, text)


def modulated_rows(image_token_activations, modulation):
    pixels = image_token_activations[0].astype(jnp.float32)
    row_mean = jnp.mean(pixels, axis=-1, keepdims=True)
    centered = pixels - row_mean
    normal_rows = centered * lax.rsqrt(
        jnp.mean(centered * centered, axis=-1, keepdims=True) + eps_norm
    )
    shift_row = modulation[0, 0].astype(jnp.float32)
    scale_row = modulation[0, 1].astype(jnp.float32)
    return (normal_rows * (1.0 + scale_row) + shift_row).astype(jnp.bfloat16)


class Gather:
    def __init__(self, weight):
        self.replicas = lax.axis_size("groups")
        self.count = lax.axis_size("seq")
        self.replica = lax.axis_index("groups")
        self.place = lax.axis_index("seq")
        self.depth = weight.shape[0]
        self.share = self.depth // self.replicas
        own = weight.transpose(1, 0, 2)
        self.whole = jnp.zeros((own.shape[0], self.depth * self.count, own.shape[2]), own.dtype)
        self.put(own, self.place * self.depth)
        piece = lax.dynamic_slice_in_dim(own, self.replica * self.share, self.share, 1)
        self.up, self.down = [piece], [piece]
        self.plan = line_plan(self.count)

    def put(self, rows, first):
        self.whole = lax.dynamic_update_slice_in_dim(self.whole, rows, first, 1)

    def travel(self):
        last = self.count - 1
        self.up.append(lax.ppermute(self.up[-1], "seq", [(i, i + 1) for i in range(last)]))
        self.down.append(lax.ppermute(self.down[-1], "seq", [(i + 1, i) for i in range(last)]))

    def pick(self, step):
        choices = {}
        for here in range(self.count):
            source, way, steps = self.plan[here][step - 1]
            choices.setdefault((way, steps), []).append(here)
        chosen = None
        for (way, steps), places in choices.items():
            array = (self.up if way == "up" else self.down)[steps]
            if chosen is None:
                chosen = array
            else:
                here = functools.reduce(jnp.logical_or, [self.place == i for i in places])
                chosen = jnp.where(here, array, chosen)
        sources = [self.plan[here][step - 1][0] for here in range(self.count)]
        return chosen, jnp.array(sources, jnp.int32)[self.place] * self.depth

    def swap(self, chosen):
        return [
            lax.ppermute(
                chosen, "groups", [((i + turn) % self.replicas, i) for i in range(self.replicas)]
            )
            for turn in range(1, self.replicas)
        ]

    def keep(self, chosen, theirs, first):
        self.put(chosen, first + self.replica * self.share)
        for turn, rows in enumerate(theirs, 1):
            replica = lax.rem(self.replica + turn, self.replicas)
            self.put(rows, first + replica * self.share)


def tied(gather, *arrays):
    held = lax.optimization_barrier((gather.up[-1], gather.down[-1]) + arrays)
    gather.up[-1], gather.down[-1] = held[:2]
    return held[2:]


def local(
    prompt_token_input,
    lengths,
    request_adapter_index,
    assignment,
    encoder_gate_weight,
    encoder_up_weight,
    encoder_down_weight,
    adapter_down_maps,
    adapter_up_maps,
    text_key_value_weight,
    image_token_activations,
    modulation,
    image_query_key_value_weight,
    query_key_norm_gain,
):
    requests = prompt_token_input.shape[0]
    positions = prompt_token_input.shape[1]
    my_slot = lax.axis_index("seq")
    steps = lax.axis_size("seq") - 1
    gather = Gather(image_query_key_value_weight)
    whole = lax.all_gather(prompt_token_input, "seq", axis=2, tiled=True)
    modulated = modulated_rows(image_token_activations, modulation)
    text_weight = text_key_value_weight.reshape(text_key_value_weight.shape[0], -1)
    whole, modulated, text_weight = tied(gather, whole, modulated, text_weight)

    full_image = lax.all_gather(modulated, "heads", axis=0, tiled=True)
    for _ in range(steps - 2):
        gather.travel()
    width = whole.shape[2]
    normed = rms_rows(whole.astype(jnp.float32)).astype(jnp.bfloat16)
    tenant_adapters = adapter_down_maps.shape[0]
    selected_adapter = (
        request_adapter_index[:, None] == jnp.arange(tenant_adapters, dtype=jnp.int32)[None, :]
    ).astype(jnp.bfloat16)
    selected_down_maps = jnp.einsum(
        "mn,nhi->mhi", selected_adapter, adapter_down_maps, preferred_element_type=jnp.float32
    ).astype(jnp.bfloat16)
    selected_up_maps = jnp.einsum(
        "zl,log->zog", selected_adapter, adapter_up_maps, preferred_element_type=jnp.float32
    ).astype(jnp.bfloat16)
    adapter_projected = jnp.einsum(
        "rpd,rdk->rpk", normed, selected_down_maps, preferred_element_type=jnp.float32
    ).astype(jnp.bfloat16)
    flattened = normed.reshape(requests * positions, width)
    gated_hidden = jnp.dot(
        flattened, encoder_gate_weight, preferred_element_type=jnp.float32
    ).reshape(requests, positions, -1)
    gated_hidden = gated_hidden + adapter_scale * jnp.einsum(
        "sqt,sti->sqi", adapter_projected, selected_up_maps, preferred_element_type=jnp.float32
    )
    up_proj = jnp.dot(flattened, encoder_up_weight, preferred_element_type=jnp.float32).reshape(
        requests, positions, -1
    )
    hidden = (jax.nn.gelu(gated_hidden, approximate=True) * up_proj).astype(jnp.bfloat16)
    slots = jnp.arange(requests, dtype=jnp.int32)
    prompt_order = jnp.sum(
        slots[None, :] * (assignment[None, :] == slots[:, None]).astype(jnp.int32), axis=1
    )
    source_row = prompt_order[my_slot]
    live_length = lengths[source_row]
    partial = jnp.einsum(
        "rpf,fd->rpd", hidden, encoder_down_weight, preferred_element_type=jnp.float32
    ).astype(jnp.bfloat16)
    partial, full_image = tied(gather, partial, full_image)

    summed = lax.psum_scatter(partial, "seq", scatter_dimension=2, tiled=True)
    gather.travel()
    waiting = []
    for step in range(1, steps - 1):
        chosen, first = gather.pick(step)
        waiting.append((chosen, gather.swap(chosen), first))
    encoded = (
        summed.astype(jnp.float32) + prompt_token_input.astype(jnp.float32)
    ).astype(jnp.bfloat16)
    (encoded,) = tied(gather, encoded)

    prompts = lax.all_gather(encoded, "heads", axis=1, tiled=True)
    gather.travel()
    chosen, first = gather.pick(steps - 1)
    waiting.append((chosen, gather.swap(chosen), first))
    for chosen, theirs, first in waiting:
        gather.keep(chosen, theirs, first)
    text_count = prompts.shape[1]
    ordered = jnp.take(prompts, prompt_order, axis=0).reshape(requests * text_count, -1)
    text_partial = (
        jnp.dot(ordered, text_weight, preferred_element_type=jnp.float32)
        .astype(jnp.bfloat16)
        .reshape(requests, text_count, -1)
    )
    text_partial, gather.whole = tied(gather, text_partial, gather.whole)

    text = lax.psum_scatter(text_partial, "seq", scatter_dimension=0, tiled=True)[0]
    chosen, first = gather.pick(steps)
    theirs = gather.swap(chosen)
    gather.keep(chosen, [], first)
    image_proj = [
        jnp.dot(full_image, gather.whole[j], preferred_element_type=jnp.float32)
        for j in range(gather.whole.shape[0])
    ]
    *theirs, held = lax.optimization_barrier((*theirs, tuple(image_proj)))
    for turn, rows in enumerate(theirs, 1):
        replica = lax.rem(gather.replica + turn, gather.replicas)
        tokens = lax.dynamic_slice_in_dim(
            full_image, first + replica * gather.share, gather.share, 1
        )
        held = [
            total + jnp.dot(tokens, rows[j], preferred_element_type=jnp.float32)
            for j, total in enumerate(held)
        ]
    image_proj = held
    output = attention(
        live_length, query_key_norm_gain, image_proj[0], image_proj[1], image_proj[2], text
    )
    return output[None]


def solution(mesh):
    return jax.shard_map(
        local,
        mesh=mesh,
        in_specs=(
            P("groups", "heads", "seq"),
            P("groups"),
            P("groups"),
            P("groups"),
            P(None, "seq"),
            P(None, "seq"),
            P("seq", None),
            P(),
            P(None, None, "seq"),
            P("seq", None, "heads"),
            P(("groups", "seq"), "heads", None),
            P(("groups", "seq"), None, None),
            P("seq", None, "heads"),
            P(None, "heads", None),
        ),
        out_specs=P(("groups", "seq"), None, "heads"),
        check_vma=False,
    )
```

```python
import functools
import math

import jax
import jax.numpy as jnp
from jax import lax
from jax.experimental import pallas as pl
from jax.experimental.pallas import tpu as pltpu
from jax.sharding import PartitionSpec as P

eps_norm = 1e-06
adapter_scale = 0.5
neg_fill = -1e30


def rms_rows(values):
    return values * lax.rsqrt(jnp.mean(values * values, axis=-1, keepdims=True) + eps_norm)


def line_plan(count):
    plan = []
    for place in range(count):
        found = []
        for steps in range(1, count):
            pair = [(place + steps, "down"), (place - steps, "up")]
            if place >= count // 2:
                pair.reverse()
            found += [(source, way, steps) for source, way in pair if 0 <= source < count]
        plan.append(found)
    return plan


def attention_kernel(
    live_ref, gain_ref, query_ref, key_ref, value_ref, text_key_ref, text_value_ref, out_ref,
    *, rows_per_step
):
    head_dim = query_ref.shape[1]
    factor = 1.0 / math.sqrt(head_dim)
    live = live_ref[0]
    image_keys = (rms_rows(key_ref[...]) * gain_ref[0, 1][None, :]).astype(jnp.bfloat16)
    text_keys = (
        rms_rows(text_key_ref[...].astype(jnp.float32)) * gain_ref[0, 2][None, :]
    ).astype(jnp.bfloat16)
    image_values = value_ref[...].astype(jnp.bfloat16)
    text_values = text_value_ref[...].astype(jnp.bfloat16)
    text_count = text_keys.shape[0]
    contract = (((1,), (1,)), ((), ()))
    for start in range(0, query_ref.shape[0], rows_per_step):
        rows = pl.ds(start, rows_per_step)
        queries = (rms_rows(query_ref[rows, :]) * gain_ref[0, 0][None, :]).astype(jnp.bfloat16)
        image_scores = lax.dot_general(
            queries, image_keys, contract, preferred_element_type=jnp.float32
        )
        text_scores = lax.dot_general(
            queries, text_keys, contract, preferred_element_type=jnp.float32
        )
        image_weights = jnp.exp(image_scores * factor)
        position = lax.broadcasted_iota(jnp.int32, (rows_per_step, text_count), 1)
        text_weights = jnp.where(position < live, jnp.exp(text_scores * factor), 0.0)
        total = jnp.sum(image_weights, axis=1, keepdims=True) + jnp.sum(
            text_weights, axis=1, keepdims=True
        )
        inverse = 1.0 / total
        attended = jnp.dot(
            (image_weights * inverse).astype(jnp.bfloat16),
            image_values,
            preferred_element_type=jnp.float32,
        ) + jnp.dot(
            (text_weights * inverse).astype(jnp.bfloat16),
            text_values,
            preferred_element_type=jnp.float32,
        )
        out_ref[rows, :] = attended.astype(out_ref.dtype)


def attention(live_length, gain, queries, keys, values, text):
    image_count, columns = queries.shape
    head_dim = gain.shape[2]
    heads_here = columns // head_dim
    text_count = text.shape[0]

    def image_block():
        return pl.BlockSpec((image_count, head_dim), lambda h: (0, h))

    rows_per_step = math.gcd(image_count, 256)
    pairs = image_count * (image_count + text_count) * heads_here
    return pl.pallas_call(
        functools.partial(attention_kernel, rows_per_step=rows_per_step),
        grid=(heads_here,),
        in_specs=[
            pl.BlockSpec(memory_space=pltpu.SMEM),
            pl.BlockSpec((1, 3, head_dim), lambda h: (h, 0, 0)),
            image_block(),
            image_block(),
            image_block(),
            pl.BlockSpec((text_count, head_dim), lambda h: (0, h)),
            pl.BlockSpec((text_count, head_dim), lambda h: (0, heads_here + h)),
        ],
        out_specs=image_block(),
        out_shape=jax.ShapeDtypeStruct((image_count, columns), jnp.bfloat16),
        compiler_params=pltpu.CompilerParams(vmem_limit_bytes=40 * 1024 * 1024),
        cost_estimate=pl.CostEstimate(
            flops=4 * pairs * head_dim,
            bytes_accessed=14 * image_count * columns + 4 * text_count * columns,
            transcendentals=pairs,
        ),
    )(live_length.reshape(1), gain.transpose(1, 0, 2), queries, keys, values, text, text)


def modulated_rows(image_token_activations, modulation):
    pixels = image_token_activations[0].astype(jnp.float32)
    row_mean = jnp.mean(pixels, axis=-1, keepdims=True)
    centered = pixels - row_mean
    normal_rows = centered * lax.rsqrt(
        jnp.mean(centered * centered, axis=-1, keepdims=True) + eps_norm
    )
    shift_row = modulation[0, 0].astype(jnp.float32)
    scale_row = modulation[0, 1].astype(jnp.float32)
    return (normal_rows * (1.0 + scale_row) + shift_row).astype(jnp.bfloat16)


class Gather:
    def __init__(self, weight):
        self.replicas = lax.axis_size("groups")
        self.count = lax.axis_size("seq")
        self.replica = lax.axis_index("groups")
        self.place = lax.axis_index("seq")
        self.depth = weight.shape[0]
        self.share = self.depth // self.replicas
        own = weight.transpose(1, 0, 2)
        self.whole = jnp.zeros((own.shape[0], self.depth * self.count, own.shape[2]), own.dtype)
        self.put(own, self.place * self.depth)
        piece = lax.dynamic_slice_in_dim(own, self.replica * self.share, self.share, 1)
        self.up, self.down = [piece], [piece]
        self.plan = line_plan(self.count)

    def put(self, rows, first):
        self.whole = lax.dynamic_update_slice_in_dim(self.whole, rows, first, 1)

    def travel(self):
        last = self.count - 1
        self.up.append(lax.ppermute(self.up[-1], "seq", [(i, i + 1) for i in range(last)]))
        self.down.append(lax.ppermute(self.down[-1], "seq", [(i + 1, i) for i in range(last)]))

    def pick(self, step):
        choices = {}
        for here in range(self.count):
            source, way, steps = self.plan[here][step - 1]
            choices.setdefault((way, steps), []).append(here)
        chosen = None
        for (way, steps), places in choices.items():
            array = (self.up if way == "up" else self.down)[steps]
            if chosen is None:
                chosen = array
            else:
                here = functools.reduce(jnp.logical_or, [self.place == i for i in places])
                chosen = jnp.where(here, array, chosen)
        sources = [self.plan[here][step - 1][0] for here in range(self.count)]
        return chosen, jnp.array(sources, jnp.int32)[self.place] * self.depth

    def swap(self, chosen):
        return [
            lax.ppermute(
                chosen, "groups", [((i + turn) % self.replicas, i) for i in range(self.replicas)]
            )
            for turn in range(1, self.replicas)
        ]

    def keep(self, chosen, theirs, first):
        self.put(chosen, first + self.replica * self.share)
        for turn, rows in enumerate(theirs, 1):
            replica = lax.rem(self.replica + turn, self.replicas)
            self.put(rows, first + replica * self.share)


def tied(gather, *arrays):
    held = lax.optimization_barrier((gather.up[-1], gather.down[-1]) + arrays)
    gather.up[-1], gather.down[-1] = held[:2]
    return held[2:]


def local(
    prompt_token_input,
    lengths,
    request_adapter_index,
    assignment,
    encoder_gate_weight,
    encoder_up_weight,
    encoder_down_weight,
    adapter_down_maps,
    adapter_up_maps,
    text_key_value_weight,
    image_token_activations,
    modulation,
    image_query_key_value_weight,
    query_key_norm_gain,
):
    requests = prompt_token_input.shape[0]
    steps = lax.axis_size("seq") - 1
    my_slot = lax.axis_index("seq")
    gather = Gather(image_query_key_value_weight)
    gathered = lax.all_gather(prompt_token_input, "heads", axis=1, tiled=True)
    positions = gathered.shape[1]
    room = requests * positions // 2
    ends = jnp.cumsum(lengths)
    starts = ends - lengths
    mine = room // lax.axis_size("heads")
    packed = lax.axis_index("heads") * mine + jnp.arange(mine, dtype=jnp.int32)
    request = jnp.minimum(
        jnp.sum((ends[None, :] <= packed[:, None]).astype(jnp.int32), axis=1), requests - 1
    )
    is_request = request[:, None] == jnp.arange(requests, dtype=jnp.int32)[None, :]

    def of_request(values):
        return jnp.sum(jnp.where(is_request, values[None, :], 0), axis=1)

    position = jnp.clip(packed - of_request(starts), 0, positions - 1)
    adapter = of_request(request_adapter_index)
    tokens_in = jnp.take(
        gathered.reshape(requests * positions, -1),
        request * positions + position,
        axis=0,
        mode="clip",
    )
    modulated = modulated_rows(image_token_activations, modulation)
    text_weight = text_key_value_weight.reshape(text_key_value_weight.shape[0], -1)
    for _ in range(steps - 2):
        gather.travel()
    tokens_in, modulated, text_weight = tied(gather, tokens_in, modulated, text_weight)

    whole = lax.all_gather(tokens_in, "seq", axis=1, tiled=True)
    whole, modulated = tied(gather, whole, modulated)

    full_image = lax.all_gather(modulated, "heads", axis=0, tiled=True)
    waiting = []
    for step in range(1, steps - 1):
        chosen, first = gather.pick(step)
        waiting.append([chosen, gather.swap(chosen), first])
    gather.travel()
    normed = rms_rows(whole.astype(jnp.float32)).astype(jnp.bfloat16)
    tenant_adapters, width, rank = adapter_down_maps.shape
    low_rank = lax.dot_general(
        normed,
        adapter_down_maps.transpose(0, 2, 1).reshape(tenant_adapters * rank, width),
        (((1,), (1,)), ((), ())),
        preferred_element_type=jnp.float32,
    ).astype(jnp.bfloat16)
    adapter_of_column = jnp.arange(tenant_adapters * rank, dtype=jnp.int32) // rank
    low_rank = jnp.where(adapter[:, None] == adapter_of_column[None, :], low_rank, 0)
    gated_hidden = jnp.dot(normed, encoder_gate_weight, preferred_element_type=jnp.float32)
    gated_hidden = gated_hidden + adapter_scale * jnp.dot(
        low_rank,
        adapter_up_maps.reshape(tenant_adapters * rank, -1),
        preferred_element_type=jnp.float32,
    )
    up_proj = jnp.dot(normed, encoder_up_weight, preferred_element_type=jnp.float32)
    hidden = (jax.nn.gelu(gated_hidden, approximate=True) * up_proj).astype(jnp.bfloat16)
    slots = jnp.arange(requests, dtype=jnp.int32)
    prompt_order = jnp.sum(
        slots[None, :] * (assignment[None, :] == slots[:, None]).astype(jnp.int32), axis=1
    )
    live_length = lengths[prompt_order[my_slot]]
    partial = jnp.dot(hidden, encoder_down_weight, preferred_element_type=jnp.float32).astype(
        jnp.bfloat16
    )
    (partial,) = tied(gather, partial)

    summed = lax.psum_scatter(partial, "seq", scatter_dimension=1, tiled=True)
    chosen, first = gather.pick(steps - 1)
    waiting.append([chosen, gather.swap(chosen), first])
    encoded = (summed.astype(jnp.float32) + tokens_in.astype(jnp.float32)).astype(jnp.bfloat16)
    (encoded,) = tied(gather, encoded)

    prompts = lax.all_gather(encoded, "heads", axis=0, tiled=True)
    gather.travel()
    text_count = positions
    offsets = jnp.arange(text_count, dtype=jnp.int32)
    rows = starts[prompt_order][:, None] + jnp.minimum(
        offsets[None, :], lengths[prompt_order][:, None] - 1
    )
    ordered = jnp.take(prompts, rows.reshape(-1), axis=0, mode="clip")
    text_partial = (
        jnp.dot(ordered, text_weight, preferred_element_type=jnp.float32)
        .astype(jnp.bfloat16)
        .reshape(requests, text_count, -1)
    )
    flat = [item for chosen, theirs, _ in waiting for item in (chosen, *theirs)]
    text_partial, full_image, *flat = tied(gather, text_partial, full_image, *flat)
    for _, theirs, first in waiting:
        gather.keep(flat[0], flat[1 : 1 + len(theirs)], first)
        flat = flat[1 + len(theirs) :]

    text = lax.psum_scatter(text_partial, "seq", scatter_dimension=0, tiled=True)[0]
    chosen, first = gather.pick(steps)
    theirs = gather.swap(chosen)
    gather.keep(chosen, [], first)
    image_proj = [
        jnp.dot(full_image, gather.whole[j], preferred_element_type=jnp.float32)
        for j in range(gather.whole.shape[0])
    ]
    *theirs, held = lax.optimization_barrier((*theirs, tuple(image_proj)))
    for turn, rows in enumerate(theirs, 1):
        replica = lax.rem(gather.replica + turn, gather.replicas)
        tokens = lax.dynamic_slice_in_dim(
            full_image, first + replica * gather.share, gather.share, 1
        )
        held = [
            total + jnp.dot(tokens, rows[j], preferred_element_type=jnp.float32)
            for j, total in enumerate(held)
        ]
    image_proj = held
    output = attention(
        live_length, query_key_norm_gain, image_proj[0], image_proj[1], image_proj[2], text
    )
    return output[None]


def solution(mesh):
    return jax.shard_map(
        local,
        mesh=mesh,
        in_specs=(
            P("groups", "heads", "seq"),
            P("groups"),
            P("groups"),
            P("groups"),
            P(None, "seq"),
            P(None, "seq"),
            P("seq", None),
            P(),
            P(None, None, "seq"),
            P("seq", None, "heads"),
            P(("groups", "seq"), "heads", None),
            P(("groups", "seq"), None, None),
            P("seq", None, "heads"),
            P(None, "heads", None),
        ),
        out_specs=P(("groups", "seq"), None, "heads"),
        check_vma=False,
    )
```

```python
import functools
import math

import jax
import jax.numpy as jnp
from jax import lax
from jax.experimental import pallas as pl
from jax.experimental.pallas import tpu as pltpu
from jax.sharding import PartitionSpec as P

eps_norm = 1e-06
adapter_scale = 0.5
neg_fill = -1e30


def rms_rows(values):
    return values * lax.rsqrt(jnp.mean(values * values, axis=-1, keepdims=True) + eps_norm)


def line_plan(count):
    plan = []
    for place in range(count):
        found = []
        for steps in range(1, count):
            pair = [(place + steps, "down"), (place - steps, "up")]
            if place >= count // 2:
                pair.reverse()
            found += [(source, way, steps) for source, way in pair if 0 <= source < count]
        plan.append(found)
    return plan


def attention_kernel(
    live_ref, gain_ref, query_ref, key_ref, value_ref, text_key_ref, text_value_ref, out_ref,
    *, rows_per_step
):
    head_dim = query_ref.shape[1]
    factor = 1.0 / math.sqrt(head_dim)
    live = live_ref[0]
    image_keys = (rms_rows(key_ref[...]) * gain_ref[0, 1][None, :]).astype(jnp.bfloat16)
    text_keys = (
        rms_rows(text_key_ref[...].astype(jnp.float32)) * gain_ref[0, 2][None, :]
    ).astype(jnp.bfloat16)
    image_values = value_ref[...].astype(jnp.bfloat16)
    text_values = text_value_ref[...].astype(jnp.bfloat16)
    text_count = text_keys.shape[0]
    contract = (((1,), (1,)), ((), ()))
    for start in range(0, query_ref.shape[0], rows_per_step):
        rows = pl.ds(start, rows_per_step)
        queries = (rms_rows(query_ref[rows, :]) * gain_ref[0, 0][None, :]).astype(jnp.bfloat16)
        image_scores = lax.dot_general(
            queries, image_keys, contract, preferred_element_type=jnp.float32
        )
        text_scores = lax.dot_general(
            queries, text_keys, contract, preferred_element_type=jnp.float32
        )
        image_weights = jnp.exp(image_scores * factor)
        position = lax.broadcasted_iota(jnp.int32, (rows_per_step, text_count), 1)
        text_weights = jnp.where(position < live, jnp.exp(text_scores * factor), 0.0)
        total = jnp.sum(image_weights, axis=1, keepdims=True) + jnp.sum(
            text_weights, axis=1, keepdims=True
        )
        inverse = 1.0 / total
        attended = jnp.dot(
            (image_weights * inverse).astype(jnp.bfloat16),
            image_values,
            preferred_element_type=jnp.float32,
        ) + jnp.dot(
            (text_weights * inverse).astype(jnp.bfloat16),
            text_values,
            preferred_element_type=jnp.float32,
        )
        out_ref[rows, :] = attended.astype(out_ref.dtype)


def attention(live_length, gain, queries, keys, values, text):
    image_count, columns = queries.shape
    head_dim = gain.shape[2]
    heads_here = columns // head_dim
    text_count = text.shape[0]

    def image_block():
        return pl.BlockSpec((image_count, head_dim), lambda h: (0, h))

    rows_per_step = math.gcd(image_count, 256)
    pairs = image_count * (image_count + text_count) * heads_here
    return pl.pallas_call(
        functools.partial(attention_kernel, rows_per_step=rows_per_step),
        grid=(heads_here,),
        in_specs=[
            pl.BlockSpec(memory_space=pltpu.SMEM),
            pl.BlockSpec((1, 3, head_dim), lambda h: (h, 0, 0)),
            image_block(),
            image_block(),
            image_block(),
            pl.BlockSpec((text_count, head_dim), lambda h: (0, h)),
            pl.BlockSpec((text_count, head_dim), lambda h: (0, heads_here + h)),
        ],
        out_specs=image_block(),
        out_shape=jax.ShapeDtypeStruct((image_count, columns), jnp.bfloat16),
        compiler_params=pltpu.CompilerParams(vmem_limit_bytes=40 * 1024 * 1024),
        cost_estimate=pl.CostEstimate(
            flops=4 * pairs * head_dim,
            bytes_accessed=14 * image_count * columns + 4 * text_count * columns,
            transcendentals=pairs,
        ),
    )(live_length.reshape(1), gain.transpose(1, 0, 2), queries, keys, values, text, text)


def modulated_rows(image_token_activations, modulation):
    pixels = image_token_activations[0].astype(jnp.float32)
    row_mean = jnp.mean(pixels, axis=-1, keepdims=True)
    centered = pixels - row_mean
    normal_rows = centered * lax.rsqrt(
        jnp.mean(centered * centered, axis=-1, keepdims=True) + eps_norm
    )
    shift_row = modulation[0, 0].astype(jnp.float32)
    scale_row = modulation[0, 1].astype(jnp.float32)
    return (normal_rows * (1.0 + scale_row) + shift_row).astype(jnp.bfloat16)


class Gather:
    def __init__(self, weight):
        self.replicas = lax.axis_size("groups")
        self.count = lax.axis_size("seq")
        self.replica = lax.axis_index("groups")
        self.place = lax.axis_index("seq")
        self.depth = weight.shape[0]
        self.share = self.depth // self.replicas
        own = weight.transpose(1, 0, 2)
        self.whole = jnp.zeros((own.shape[0], self.depth * self.count, own.shape[2]), own.dtype)
        self.put(own, self.place * self.depth)
        piece = lax.dynamic_slice_in_dim(own, self.replica * self.share, self.share, 1)
        self.up, self.down = [piece], [piece]
        self.plan = line_plan(self.count)

    def put(self, rows, first):
        self.whole = lax.dynamic_update_slice_in_dim(self.whole, rows, first, 1)

    def travel(self):
        last = self.count - 1
        self.up.append(lax.ppermute(self.up[-1], "seq", [(i, i + 1) for i in range(last)]))
        self.down.append(lax.ppermute(self.down[-1], "seq", [(i + 1, i) for i in range(last)]))

    def pick(self, step):
        choices = {}
        for here in range(self.count):
            source, way, steps = self.plan[here][step - 1]
            choices.setdefault((way, steps), []).append(here)
        chosen = None
        for (way, steps), places in choices.items():
            array = (self.up if way == "up" else self.down)[steps]
            if chosen is None:
                chosen = array
            else:
                here = functools.reduce(jnp.logical_or, [self.place == i for i in places])
                chosen = jnp.where(here, array, chosen)
        sources = [self.plan[here][step - 1][0] for here in range(self.count)]
        return chosen, jnp.array(sources, jnp.int32)[self.place] * self.depth

    def swap(self, chosen):
        return [
            lax.ppermute(
                chosen, "groups", [((i + turn) % self.replicas, i) for i in range(self.replicas)]
            )
            for turn in range(1, self.replicas)
        ]

    def keep(self, chosen, theirs, first):
        self.put(chosen, first + self.replica * self.share)
        for turn, rows in enumerate(theirs, 1):
            replica = lax.rem(self.replica + turn, self.replicas)
            self.put(rows, first + replica * self.share)


def tied(gather, *arrays):
    held = lax.optimization_barrier((gather.up[-1], gather.down[-1]) + arrays)
    gather.up[-1], gather.down[-1] = held[:2]
    return held[2:]


def local(
    prompt_token_input,
    lengths,
    request_adapter_index,
    assignment,
    encoder_gate_weight,
    encoder_up_weight,
    encoder_down_weight,
    adapter_down_maps,
    adapter_up_maps,
    text_key_value_weight,
    image_token_activations,
    modulation,
    image_query_key_value_weight,
    query_key_norm_gain,
):
    requests = prompt_token_input.shape[0]
    steps = lax.axis_size("seq") - 1
    my_slot = lax.axis_index("seq")
    gather = Gather(image_query_key_value_weight)
    gathered = lax.all_gather(prompt_token_input, "heads", axis=1, tiled=True)
    positions = gathered.shape[1]
    room = requests * positions // 2
    ends = jnp.cumsum(lengths)
    starts = ends - lengths
    mine = room // lax.axis_size("heads")
    packed = lax.axis_index("heads") * mine + jnp.arange(mine, dtype=jnp.int32)
    request = jnp.minimum(
        jnp.sum((ends[None, :] <= packed[:, None]).astype(jnp.int32), axis=1), requests - 1
    )
    is_request = request[:, None] == jnp.arange(requests, dtype=jnp.int32)[None, :]

    def of_request(values):
        return jnp.sum(jnp.where(is_request, values[None, :], 0), axis=1)

    position = jnp.clip(packed - of_request(starts), 0, positions - 1)
    adapter = of_request(request_adapter_index)
    tokens_in = jnp.take(
        gathered.reshape(requests * positions, -1),
        request * positions + position,
        axis=0,
        mode="clip",
    )
    modulated = modulated_rows(image_token_activations, modulation)
    text_weight = text_key_value_weight.reshape(text_key_value_weight.shape[0], -1)
    for _ in range(steps - 2):
        gather.travel()
    tokens_in, modulated, text_weight = tied(gather, tokens_in, modulated, text_weight)

    whole = lax.all_gather(tokens_in, "seq", axis=1, tiled=True)
    whole, modulated, gather.whole = tied(gather, whole, modulated, gather.whole)

    full_image = lax.all_gather(modulated, "heads", axis=0, tiled=True)
    waiting = []
    for step in range(1, steps - 1):
        chosen, first = gather.pick(step)
        waiting.append([chosen, gather.swap(chosen), first])
    gather.travel()
    normed = rms_rows(whole.astype(jnp.float32)).astype(jnp.bfloat16)
    tenant_adapters, width, rank = adapter_down_maps.shape
    low_rank = lax.dot_general(
        normed,
        adapter_down_maps.transpose(0, 2, 1).reshape(tenant_adapters * rank, width),
        (((1,), (1,)), ((), ())),
        preferred_element_type=jnp.float32,
    ).astype(jnp.bfloat16)
    adapter_of_column = jnp.arange(tenant_adapters * rank, dtype=jnp.int32) // rank
    low_rank = jnp.where(adapter[:, None] == adapter_of_column[None, :], low_rank, 0)
    gated_hidden = jnp.dot(normed, encoder_gate_weight, preferred_element_type=jnp.float32)
    gated_hidden = gated_hidden + adapter_scale * jnp.dot(
        low_rank,
        adapter_up_maps.reshape(tenant_adapters * rank, -1),
        preferred_element_type=jnp.float32,
    )
    up_proj = jnp.dot(normed, encoder_up_weight, preferred_element_type=jnp.float32)
    hidden = (jax.nn.gelu(gated_hidden, approximate=True) * up_proj).astype(jnp.bfloat16)
    slots = jnp.arange(requests, dtype=jnp.int32)
    prompt_order = jnp.sum(
        slots[None, :] * (assignment[None, :] == slots[:, None]).astype(jnp.int32), axis=1
    )
    live_length = lengths[prompt_order[my_slot]]
    partial = jnp.dot(hidden, encoder_down_weight, preferred_element_type=jnp.float32).astype(
        jnp.bfloat16
    )
    partial, full_image, waiting = tied(gather, partial, full_image, waiting)
    for chosen, theirs, first in waiting:
        gather.keep(chosen, theirs, first)

    summed = lax.psum_scatter(partial, "seq", scatter_dimension=1, tiled=True)
    chosen, first = gather.pick(steps - 1)
    theirs = gather.swap(chosen)
    encoded = (summed.astype(jnp.float32) + tokens_in.astype(jnp.float32)).astype(jnp.bfloat16)
    encoded, gather.whole = tied(gather, encoded, gather.whole)

    prompts = lax.all_gather(encoded, "heads", axis=0, tiled=True)
    gather.travel()
    text_count = positions
    offsets = jnp.arange(text_count, dtype=jnp.int32)
    rows = starts[prompt_order][:, None] + jnp.minimum(
        offsets[None, :], lengths[prompt_order][:, None] - 1
    )
    ordered = jnp.take(prompts, rows.reshape(-1), axis=0, mode="clip")
    text_partial = (
        jnp.dot(ordered, text_weight, preferred_element_type=jnp.float32)
        .astype(jnp.bfloat16)
        .reshape(requests, text_count, -1)
    )
    text_partial, chosen, theirs = tied(gather, text_partial, chosen, theirs)
    gather.keep(chosen, theirs, first)

    text = lax.psum_scatter(text_partial, "seq", scatter_dimension=0, tiled=True)[0]
    chosen, first = gather.pick(steps)
    theirs = gather.swap(chosen)
    gather.keep(chosen, [], first)
    image_proj = [
        jnp.dot(full_image, gather.whole[j], preferred_element_type=jnp.float32)
        for j in range(gather.whole.shape[0])
    ]
    *theirs, held = lax.optimization_barrier((*theirs, tuple(image_proj)))
    for turn, rows in enumerate(theirs, 1):
        replica = lax.rem(gather.replica + turn, gather.replicas)
        tokens = lax.dynamic_slice_in_dim(
            full_image, first + replica * gather.share, gather.share, 1
        )
        held = [
            total + jnp.dot(tokens, rows[j], preferred_element_type=jnp.float32)
            for j, total in enumerate(held)
        ]
    image_proj = held
    output = attention(
        live_length, query_key_norm_gain, image_proj[0], image_proj[1], image_proj[2], text
    )
    return output[None]


def solution(mesh):
    return jax.shard_map(
        local,
        mesh=mesh,
        in_specs=(
            P("groups", "heads", "seq"),
            P("groups"),
            P("groups"),
            P("groups"),
            P(None, "seq"),
            P(None, "seq"),
            P("seq", None),
            P(),
            P(None, None, "seq"),
            P("seq", None, "heads"),
            P(("groups", "seq"), "heads", None),
            P(("groups", "seq"), None, None),
            P("seq", None, "heads"),
            P(None, "heads", None),
        ),
        out_specs=P(("groups", "seq"), None, "heads"),
        check_vma=False,
    )
```
